32 devices in a mesh: img: 8 (over y, x, core), cls: 4 (over z).
Axes of the slice: x: 2, y: 2, z: 4, core: 2. Of those that a mesh axis runs over, the one named last changes fastest.
Arguments:
- images: float32 [256, 6144], P('img'), may hold values from -64 to 64
- classes: float32 [1024, 6144], P('cls'), may hold values from -1.2 to 1.2
- groups: int32 [256], P('img'), may hold values from 0 to 63
- ctf: float32 [64, 48], replicated, may hold values from -1 to 1
- noise_weight: float32 [48], replicated, may hold values from 1 to 4
- cycle_prior: float32 [48], replicated, may hold values from 0.5 to 4
Outputs:
- classes_out: float32 [1024, 6144], P('cls')
- log_evidence: float32 [256], P('img')
The draws below stay inside these ranges and needn't reach their ends.
All inputs are finite; a program needn't handle non-finite values.
Results may differ from the reference program's by a relative error of at most 0.0003.
Values sent between devices are 32-bit elements; how exact they have to be, the bound alone decides.
No kernel may reach another device: no remote copies, remote signals or barrier semaphores. Data moves between devices by JAX's collectives and lax.ppermute only.
A program may use at most 128 MiB of HBM per device.

```python
import math
import jax
import jax.numpy as jnp
from jax import lax

IMG_DEV = 32
K = 1024
R = 48
F = 64
J = 384
G = 64
ITERS = 2
IMAGES = 256
N_IMG = 8


def class_field(key, spread):
    key = jax.random.fold_in(key, 101)
    size_key, angle_key = jax.random.split(key)
    modulus = jax.random.uniform(size_key, (K, F, R), jnp.float32, 1.0 - spread, 1.0 + spread)
    angle = jax.random.uniform(angle_key, (K, F, R), jnp.float32, -math.pi, math.pi)
    return jnp.stack([modulus * jnp.cos(angle), modulus * jnp.sin(angle)], axis=2)


def group_labels(key):
    key = jax.random.fold_in(key, 102)
    return jax.random.randint(key, (IMAGES,), 0, G, jnp.int32)


def ctf_table(key):
    key = jax.random.fold_in(key, 103)
    sign_key, size_key = jax.random.split(key)
    signs = jnp.where(jax.random.bernoulli(sign_key, 0.5, (G, R)), 1.0, -1.0).astype(jnp.float32)
    return signs * jax.random.uniform(size_key, (G, R), jnp.float32, 0.2, 1.0)


def draw_classes(key, part):
    spread = 0.15
    return class_field(key, spread).reshape(K, F * 2 * R)


def draw_groups(key, part):
    return group_labels(key)


def draw_ctf(key, part):
    return ctf_table(key)


def draw_images(key, part):
    spread = 0.15
    field = class_field(key, spread)
    labels = group_labels(key)
    table = ctf_table(key)
    key = jax.random.fold_in(key, 11)
    keys = jax.random.split(key, 5)
    chosen = jax.random.randint(keys[0], (IMAGES,), 0, K, jnp.int32)
    turned = jax.random.randint(keys[1], (IMAGES,), 0, J, jnp.int32)
    orders = jnp.arange(F, dtype=jnp.int32)
    residue = turned[:, None] * orders[None, :] % J
    phases = residue.astype(jnp.float32) * (2.0 * math.pi / J)
    cosine = jnp.cos(phases)[:, :, None]
    sine = jnp.sin(phases)[:, :, None]
    source = field[chosen]
    real_part = source[:, :, 0] * cosine + source[:, :, 1] * sine
    imag_part = source[:, :, 1] * cosine - source[:, :, 0] * sine
    rotated = jnp.stack([real_part, imag_part], axis=2) * table[labels][:, None, None, :]
    strength = jnp.exp(jax.random.uniform(keys[2], (IMAGES, 1, 1, 1), jnp.float32, math.log(0.01), math.log(0.25)))
    level = jnp.exp(jax.random.uniform(keys[3], (IMAGES, 1, 1, 1), jnp.float32, math.log(0.15), math.log(0.6)))
    noise = jax.random.truncated_normal(keys[4], -4.0, 4.0, (IMAGES, F, 2, R), jnp.float32)
    values = rotated * strength + level * noise
    return jnp.clip(values.reshape(IMAGES, F * 2 * R), -64.0, 64.0)


def setup_inputs(seed: int = 0) -> dict:
    key_list = jax.random.split(jax.random.key(seed), 7)
    images = draw_images(jax.random.fold_in(key_list[6], 71), 0)
    classes = draw_classes(jax.random.fold_in(key_list[6], 71), 0)
    groups = draw_groups(jax.random.fold_in(key_list[6], 71), 0)
    ctf = draw_ctf(jax.random.fold_in(key_list[6], 71), 0)
    noise_weight = jnp.clip(jnp.exp(jax.random.uniform(key_list[4], (R,), jnp.float32, math.log(1.0), math.log(4.0))), 1.0, 4.0)
    cycle_prior = jnp.clip(jnp.exp(jax.random.uniform(key_list[5], (R,), jnp.float32, math.log(0.5), math.log(4.0))), 0.5, 4.0)
    return {"images": images, "classes": classes, "groups": groups, "ctf": ctf, "noise_weight": noise_weight, "cycle_prior": cycle_prior}


highest = lax.Precision.HIGHEST

def phase_tables():
    orders = jnp.arange(F, dtype=jnp.int32)
    rotation = jnp.arange(J, dtype=jnp.int32)
    residue = orders[:, None] * rotation[None, :] % J
    phases = residue.astype(jnp.float32) * (2.0 * math.pi / J)
    harmonic = jnp.where(orders == 0, 1.0, 2.0).astype(jnp.float32)
    score_table = jnp.stack([harmonic[:, None] * jnp.cos(phases), -harmonic[:, None] * jnp.sin(phases)])
    back_table = jnp.stack([jnp.cos(phases), jnp.sin(phases)])
    return (harmonic, score_table, back_table)

def image_ctf(labels, ctf):
    onehot = (labels[:, None] == jnp.arange(G, dtype=jnp.int32)[None, :]).astype(jnp.float32)
    return (onehot, jnp.dot(onehot, ctf, precision=highest))

def class_scores(pixels, onehot, ctf_rows, weights, current, ctf, harmonic, score_table):
    scaled = pixels * (ctf_rows * weights[None, :])[:, None, None, :]
    turned = jnp.stack([scaled[:, :, 1], -scaled[:, :, 0]], axis=2)
    paired = jnp.stack([scaled, turned], axis=1)
    correlation = jnp.einsum('nqmpr,kmpr->nkqm', paired, current, precision=highest)
    class_power = jnp.einsum('m,kmpr->kr', harmonic, current * current, precision=highest)
    group_penalty = jnp.dot(ctf * ctf * weights[None, :], class_power.T, precision=highest)
    penalty = jnp.dot(onehot, group_penalty, precision=highest)
    return jnp.einsum('nkqm,qmj->nkj', correlation, score_table, precision=highest) - 0.5 * penalty[:, :, None]

def class_terms(pixels, ctf_rows, posterior, back_table):
    phasor = jnp.einsum('nkj,qmj->nkqm', posterior, back_table, precision=highest)
    carried = pixels * ctf_rows[:, None, None, :]
    turned = jnp.stack([-carried[:, :, 1], carried[:, :, 0]], axis=2)
    spread_pixels = jnp.stack([carried, turned], axis=1)
    numerator = jnp.einsum('nkqm,nqmpr->kmpr', phasor, spread_pixels, precision=highest)
    image_mass = lax.optimization_barrier(jnp.sum(posterior, axis=2))
    weight_sum = jnp.dot(image_mass.T, ctf_rows * ctf_rows, precision=highest)
    return (numerator, weight_sum)

def reference(images, classes, groups, ctf, noise_weight, cycle_prior):
    harmonic, score_table, back_table = phase_tables()
    weights = noise_weight / math.sqrt(F * R)
    current = classes.reshape(K, F, 2, R)
    pixel_blocks = images.reshape(N_IMG, IMG_DEV, F, 2, R)
    label_blocks = groups.reshape(N_IMG, IMG_DEV)
    evidence = jnp.zeros((N_IMG, IMG_DEV), jnp.float32)
    for iteration in range(ITERS):

        def accumulate(running, block_data, current=current):
            pixels, labels = block_data
            onehot, ctf_rows = image_ctf(labels, ctf)
            scores = class_scores(pixels, onehot, ctf_rows, weights, current, ctf, harmonic, score_table)
            largest = lax.optimization_barrier(jnp.max(scores, axis=(1, 2)))
            weighted = jnp.exp(scores - largest[:, None, None])
            normaliser = lax.optimization_barrier(jnp.sum(weighted, axis=(1, 2)))
            posterior = weighted / normaliser[:, None, None]
            numerator, weight_sum = class_terms(pixels, ctf_rows, posterior, back_table)
            return ((running[0] + numerator, running[1] + weight_sum), largest + jnp.log(normaliser))
        initial = (jnp.zeros((K, F, 2, R), jnp.float32), jnp.zeros((K, R), jnp.float32))
        (numerator, weight_sum), evidence = lax.scan(accumulate, initial, (pixel_blocks, label_blocks))
        current = (numerator + cycle_prior * current) / (weight_sum[:, None, None, :] + cycle_prior)
    return (current.reshape(K, F * 2 * R), evidence.reshape(IMAGES))
```

```python
import math

import jax
import jax.numpy as jnp
import numpy as np
from jax import lax
from jax.experimental import pallas as pl
from jax.experimental.pallas import tpu as pltpu
from jax.sharding import PartitionSpec as P

R = 48
F = 64
J = 384
G = 64
LANES = 128
ITERS = 2
HALF = J // 2
PAIR = 2 * R
GROUP = 4 * PAIR
LOG2E = math.log2(math.e)
LN2 = math.log(2.0)
VMEM_BYTES = 56 * 1024 * 1024

highest = lax.Precision.HIGHEST
f32 = jnp.float32
bf16 = jnp.bfloat16


def split(value):
    high = value.astype(bf16)
    return high, (value - high.astype(f32)).astype(bf16)


def split_table(table):
    high = table.astype(jnp.bfloat16)
    return high, (table - high.astype(np.float32)).astype(jnp.bfloat16)


def make_tables():
    turn = np.arange(HALF)
    score, back = [], []
    for parity in range(2):
        orders = np.arange(parity, F, 2)
        phase = (orders[:, None] * turn[None, :] % J) * (2.0 * math.pi / J)
        harmonic = np.where(orders == 0, 1.0, 2.0)[:, None] * LOG2E
        rows = np.stack([harmonic * np.cos(phase), -harmonic * np.sin(phase)], 1).reshape(F, HALF)
        high, low = split_table(rows.T.astype(np.float32))
        score.append(np.concatenate([high, high, low], 1))
        rows = np.stack([np.cos(phase), np.sin(phase)], 1).reshape(F, HALF).astype(np.float32)
        high, low = split_table(rows)
        back.append(np.concatenate([high, low], 0))
    return np.stack(score), np.stack(back)


def dot(a, b):
    return jnp.dot(a, b, preferred_element_type=f32)


def dot_nt(a, b):
    return lax.dot_general(a, b, (((1,), (1,)), ((), ())), preferred_element_type=f32)


def quarter_turn(value, sign):
    return jnp.concatenate([-sign * value[:, R:], sign * value[:, :R]], axis=1)


def prepare_kernel(images_ref, ctf_ref, high_ref, low_ref):
    turned = images_ref[...].T
    scale = jnp.concatenate([ctf_ref[...]] * (GROUP // R), axis=0)
    high, low = split(turned * scale)
    high_ref[...] = high
    low_ref[...] = low


def prepare(images, ctf_turned):
    count, width = images.shape
    return pl.pallas_call(
        prepare_kernel,
        grid=(width // GROUP,),
        in_specs=[
            pl.BlockSpec((count, GROUP), lambda i: (0, i)),
            pl.BlockSpec((R, count), lambda i: (0, 0)),
        ],
        out_specs=[pl.BlockSpec((GROUP, count), lambda i: (i, 0))] * 2,
        out_shape=[jax.ShapeDtypeStruct((width, count), bf16)] * 2,
        compiler_params=pltpu.CompilerParams(vmem_limit_bytes=VMEM_BYTES),
        name="prepare",
    )(images, ctf_turned)


def row_of(order_pair, parity, q):
    return parity * F + order_pair * 2 + q


def score_kernel(
    classes_ref, weight_ref, penalty_ref, high_ref, low_ref, score_ref, back_ref,
    phasor_ref, peak_ref, total_ref, stat_ref, corr_ref,
):
    number = classes_ref.shape[0]

    def correlate(block, _):
        scaled = classes_ref[:, pl.ds(pl.multiple_of(block * GROUP, GROUP), GROUP)] * weight_ref[...]
        for i in range(4):
            own = scaled[:, i * PAIR : (i + 1) * PAIR]
            lhs_high, lhs_low = split(jnp.concatenate([own, quarter_turn(own, 1.0)], axis=0))
            rows = pl.ds(pl.multiple_of(block * GROUP + i * PAIR, PAIR), PAIR)
            high = high_ref[rows, :]
            out = dot(jnp.concatenate([lhs_high, lhs_low], axis=0), high)
            out = out[: 2 * number] + out[2 * number :] + dot(lhs_high, low_ref[rows, :])
            for q in range(2):
                start = row_of(block * 2 + i // 2, i % 2, q)
                for side in range(corr_ref.shape[0]):
                    lanes = slice(side * LANES, (side + 1) * LANES)
                    corr_ref[side, pl.ds(start, number, stride=2 * F), :] = out[q * number : (q + 1) * number, lanes]
        return 0

    lax.fori_loop(0, F // 4, correlate, 0)

    def rotate(k, _):
        waves = []
        for parity in range(2):
            rows = pl.ds(pl.multiple_of(k * 2 * F + parity * F, F), F)
            corr = jnp.concatenate([corr_ref[side, rows, :] for side in range(corr_ref.shape[0])], axis=1)
            high, low = split(corr)
            waves.append(dot(score_ref[parity], jnp.concatenate([high, low, high], axis=0)))
        even, odd = waves
        peak = jnp.max(even + jnp.abs(odd), axis=0, keepdims=True)
        base = even - peak
        first = jnp.exp2(base + odd)
        second = jnp.exp2(base - odd)
        plus = first + second
        minus = first - second
        for parity, folded in enumerate((plus, minus)):
            high, low = split(folded)
            out = dot(back_ref[parity], high)
            out = out[:F] + out[F:] + dot(back_ref[parity, :F], low)
            rows = pl.ds(pl.multiple_of(k * 2 * F + parity * F, F), F)
            for side in range(phasor_ref.shape[0]):
                phasor_ref[side, rows, :] = out[:, side * LANES : (side + 1) * LANES]
        peak_ref[pl.ds(k, 1), :] = peak - penalty_ref[pl.ds(k, 1), :]
        total_ref[pl.ds(k, 1), :] = jnp.sum(plus, axis=0, keepdims=True)
        return 0

    lax.fori_loop(0, number, rotate, 0)
    largest = jnp.max(peak_ref[...], axis=0, keepdims=True)
    stat_ref[0:1, :] = largest
    stat_ref[1:2, :] = jnp.sum(total_ref[...] * jnp.exp2(peak_ref[...] - largest), axis=0, keepdims=True)


def score(classes, weight_row, penalty, high, low, score_table, back_table):
    number, width = classes.shape
    count = high.shape[1]
    return pl.pallas_call(
        score_kernel,
        out_shape=[
            jax.ShapeDtypeStruct((count // LANES, number * 2 * F, LANES), f32),
            jax.ShapeDtypeStruct((number, count), f32),
            jax.ShapeDtypeStruct((number, count), f32),
            jax.ShapeDtypeStruct((2, count), f32),
        ],
        scratch_shapes=[pltpu.VMEM((count // LANES, number * 2 * F, LANES), f32)],
        compiler_params=pltpu.CompilerParams(vmem_limit_bytes=VMEM_BYTES),
        name="score",
    )(classes, weight_row, penalty, high, low, score_table, back_table)


def update_kernel(
    classes_ref, phasor_ref, peak_ref, total_ref, joint_ref, high_ref, low_ref, square_ref, prior_ref, out_ref
):
    number = classes_ref.shape[0]
    factor = jnp.exp2(peak_ref[...] - joint_ref[0:1, :]) * (1.0 / joint_ref[1:2, :])
    mass = total_ref[...] * factor
    weight = lax.dot_general(
        mass, square_ref[...], (((1,), (1,)), ((), ())), precision=highest, preferred_element_type=f32
    )
    scale = 1.0 / (weight + prior_ref[:, :R])
    scale = jnp.concatenate([scale] * (GROUP // R), axis=1)

    def update(block, _):
        parts = []
        for i in range(4):
            lhs = []
            for q in range(2):
                start = row_of(block * 2 + i // 2, i % 2, q)
                rows = pl.ds(start, number, stride=2 * F)
                sides = [phasor_ref[side, rows, :] for side in range(phasor_ref.shape[0])]
                lhs.append(jnp.concatenate(sides, axis=1) * factor)
            lhs_high, lhs_low = split(jnp.concatenate(lhs, axis=0))
            rows = pl.ds(pl.multiple_of(block * GROUP + i * PAIR, PAIR), PAIR)
            out = dot_nt(jnp.concatenate([lhs_high, lhs_low], axis=0), high_ref[rows, :])
            out = out[: 2 * number] + out[2 * number :] + dot_nt(lhs_high, low_ref[rows, :])
            parts.append(out[:number] + quarter_turn(out[number:], 1.0))
        columns = pl.ds(pl.multiple_of(block * GROUP, GROUP), GROUP)
        numerator = jnp.concatenate(parts, axis=1)
        out_ref[:, columns] = (numerator + prior_ref[...] * classes_ref[:, columns]) * scale
        return 0

    lax.fori_loop(0, F // 4, update, 0)


def update(classes, phasor, peak, total, joint, high, low, square, prior_row):
    return pl.pallas_call(
        update_kernel,
        out_shape=jax.ShapeDtypeStruct(classes.shape, f32),
        compiler_params=pltpu.CompilerParams(vmem_limit_bytes=VMEM_BYTES),
        name="update",
    )(classes, phasor, peak, total, joint, high, low, square, prior_row)


def flipped(array, axis, bit):
    size = lax.axis_size(axis)
    return lax.ppermute(array, axis, [(i, i ^ bit) for i in range(size)])


def gather_blocks(block, me):
    rows = block.shape[0]
    half = rows // 2
    beside = flipped(block, "img", 2)
    above = flipped(block, "img", 4)
    top = flipped(beside[:half], "img", 4)
    bottom = flipped(above[half:], "img", 2)
    mine = jnp.concatenate([block, beside, above, top, bottom], axis=0)
    other = flipped(mine, "img", 1)
    out = jnp.zeros((8 * rows,) + block.shape[1:], block.dtype)
    for step in range(4):
        piece = slice(step * rows, (step + 1) * rows)
        out = lax.dynamic_update_slice(out, mine[piece], ((me ^ (2 * step)) * rows, 0))
        out = lax.dynamic_update_slice(out, other[piece], ((me ^ (2 * step + 1)) * rows, 0))
    return out


def combine(earlier, latter):
    largest = jnp.maximum(earlier[0:1], latter[0:1])
    summed = earlier[1:2] * jnp.exp2(earlier[0:1] - largest) + latter[1:2] * jnp.exp2(latter[0:1] - largest)
    return jnp.concatenate([largest, summed], axis=0)


def join(stat):
    for axis in ("img", "cls"):
        bit = 1
        while bit < lax.axis_size(axis):
            stat = combine(stat, flipped(stat, axis, bit))
            bit *= 2
    return stat


def per_device(images, classes, groups, ctf, noise_weight, cycle_prior):
    score_table, back_table = make_tables()
    score_table, back_table = jnp.asarray(score_table), jnp.asarray(back_table)
    weights = noise_weight / math.sqrt(F * R)
    me = lax.axis_index("img")
    local = images.shape[0]
    number = classes.shape[0] // lax.axis_size("img")
    all_images = gather_blocks(images, me)
    all_groups = lax.all_gather(groups.astype(f32), "img", tiled=True)
    onehot = (all_groups[:, None] == jnp.arange(G, dtype=f32)[None, :]).astype(f32)
    ctf_turned = lax.dot_general(ctf, onehot, (((0,), (1,)), ((), ())), precision=highest)
    square = ctf_turned * ctf_turned
    high, low = prepare(all_images, ctf_turned)
    current = lax.dynamic_slice_in_dim(classes, me * number, number, 0)
    weight_row = jnp.tile(weights, GROUP // R)[None, :]
    prior_row = jnp.tile(cycle_prior, GROUP // R)[None, :]
    harmonic = jnp.where(jnp.arange(F) == 0, 1.0, 2.0).astype(f32)
    penalty_table = square * (0.5 * LOG2E) * weights[:, None]
    for iteration in range(ITERS):
        power = jnp.einsum("kmpr,m->kr", (current * current).reshape(number, F, 2, R), harmonic, precision=highest)
        penalty = jnp.dot(power, penalty_table, precision=highest)
        phasor, peak, total, stat = score(current, weight_row, penalty, high, low, score_table, back_table)
        joint = join(stat)
        current = update(current, phasor, peak, total, joint, high, low, square, prior_row)
    mine = lax.dynamic_slice_in_dim(joint, me * local, local, 1)
    evidence = mine[0] * LN2 + jnp.log(mine[1])
    return gather_blocks(current, me), evidence


def joined(part, axis, combine):
    gathered = jax.tree.map(lambda a: lax.all_gather(a, axis), part)

    def take(source):
        return jax.tree.map(lambda a: lax.dynamic_index_in_dim(a, source, 0, False), gathered)

    return lax.fori_loop(
        1, lax.axis_size(axis), lambda source, state: combine(state, take(source)), take(0)
    )


def phase_tables():
    orders = jnp.arange(F, dtype=jnp.int32)
    rotation = jnp.arange(J, dtype=jnp.int32)
    residue = orders[:, None] * rotation[None, :] % J
    phases = residue.astype(jnp.float32) * (2.0 * math.pi / J)
    harmonic = jnp.where(orders == 0, 1.0, 2.0).astype(jnp.float32)
    score_table = jnp.stack(
        [harmonic[:, None] * jnp.cos(phases), -harmonic[:, None] * jnp.sin(phases)]
    )
    back_table = jnp.stack([jnp.cos(phases), jnp.sin(phases)])
    return (harmonic, score_table, back_table)


def image_ctf(labels, ctf):
    onehot = (labels[:, None] == jnp.arange(G, dtype=jnp.int32)[None, :]).astype(jnp.float32)
    return (onehot, jnp.dot(onehot, ctf, precision=highest))


def class_scores(pixels, onehot, ctf_rows, weights, current, ctf, harmonic, score_table):
    scaled = pixels * (ctf_rows * weights[None, :])[:, None, None, :]
    turned = jnp.stack([scaled[:, :, 1], -scaled[:, :, 0]], axis=2)
    paired = jnp.stack([scaled, turned], axis=1)
    correlation = jnp.einsum("nqmpr,kmpr->nkqm", paired, current, precision=highest)
    class_power = jnp.einsum("m,kmpr->kr", harmonic, current * current, precision=highest)
    group_penalty = jnp.dot(ctf * ctf * weights[None, :], class_power.T, precision=highest)
    penalty = jnp.dot(onehot, group_penalty, precision=highest)
    return (
        jnp.einsum("nkqm,qmj->nkj", correlation, score_table, precision=highest)
        - 0.5 * penalty[:, :, None]
    )


def class_terms(pixels, ctf_rows, posterior, back_table):
    phasor = jnp.einsum("nkj,qmj->nkqm", posterior, back_table, precision=highest)
    carried = pixels * ctf_rows[:, None, None, :]
    turned = jnp.stack([-carried[:, :, 1], carried[:, :, 0]], axis=2)
    spread_pixels = jnp.stack([carried, turned], axis=1)
    numerator = jnp.einsum("nkqm,nqmpr->kmpr", phasor, spread_pixels, precision=highest)
    image_mass = jnp.sum(posterior, axis=2)
    weight_sum = jnp.dot(image_mass.T, ctf_rows * ctf_rows, precision=highest)
    return (numerator, weight_sum)


def combine_peaks(earlier, latter):
    largest = jnp.maximum(earlier[0], latter[0])
    summed = earlier[1] * jnp.exp(earlier[0] - largest) + latter[1] * jnp.exp(latter[0] - largest)
    return (largest, summed)


def plain_device(images, classes, groups, ctf, noise_weight, cycle_prior):
    harmonic, score_table, back_table = phase_tables()
    weights = noise_weight / math.sqrt(F * R)
    local_images = images.shape[0]
    local_classes = classes.shape[0]
    pixels = images.reshape(local_images, F, 2, R)
    current = classes.reshape(local_classes, F, 2, R)
    onehot, ctf_rows = image_ctf(groups, ctf)
    for iteration in range(ITERS):
        scores = class_scores(
            pixels, onehot, ctf_rows, weights, current, ctf, harmonic, score_table
        )
        local_peak = jnp.max(scores, axis=(1, 2))
        weighted = jnp.exp(scores - local_peak[:, None, None])
        local_total = jnp.sum(weighted, axis=(1, 2))
        largest, normaliser = joined((local_peak, local_total), "cls", combine_peaks)
        posterior = weighted * (jnp.exp(local_peak - largest) / normaliser)[:, None, None]
        numerator, weight_sum = class_terms(pixels, ctf_rows, posterior, back_table)
        whole_numerator, whole_weight = lax.psum((numerator, weight_sum), "img")
        current = (whole_numerator + cycle_prior * current) / (
            whole_weight[:, None, None, :] + cycle_prior
        )
    return (current.reshape(local_classes, F * 2 * R), largest + jnp.log(normaliser))


def solution(mesh):
    in_specs = (P("img", None), P("cls", None), P("img"), P(), P(), P())
    out_specs = (P("cls", None), P("img"))
    planned = per_device if mesh.shape["img"] == 8 else plain_device
    return jax.shard_map(
        planned, mesh=mesh, in_specs=in_specs, out_specs=out_specs, check_vma=False
    )
```
